32 devices in a mesh: dp: 4 (over x, core), blk: 8 (over z, y).
Axes of the slice: x: 2, y: 2, z: 4, core: 2. Of those that a mesh axis runs over, the one named last changes fastest.
Arguments:
- rows: bfloat16 [32768, 768], P(('dp', 'blk')), may hold values from -6 to 6
- block_ids: int32 [32768, 1], P(('dp', 'blk')), may hold values from 0 to 31; in each aligned block of 1024 rows (0 to 1023, 1024 to 2047, ...) at most 64 rows name the same one
- centroids: float32 [32768, 768], P(('dp', 'blk')), may hold values from -6 to 6
- pairing: int32 [2], replicated, may hold values from 1 to 7
Outputs:
- centers: float32 [32768, 768], P(('dp', 'blk'))
- energy: float32 [32768], P(('dp', 'blk'))
The draws below stay inside these ranges and needn't reach their ends.
Inputs may be any that keep to these rules, and one draw needn't show every extreme that they name: Row r belongs to the block owned by the device of flat index block_ids[r, 0] over dp+blk with dp slowest; among the rows of one device no id occurs more than 64 times, and that many is reached in every draw. In pass p, the blocks at positions k and k XOR pairing[p] of one group are partners.
All inputs are finite; a program needn't handle non-finite values.
Results may differ from the reference program's by a relative error of at most 0.007.
Values may be sent and summed in bfloat16 or wider, within the bound.
A program may use at most 64 MiB of HBM per device.

```python
import math
import jax
import jax.numpy as jnp
import numpy as np
from jax import lax

D = 768
C_DEV = 1024
ROWS_DEV = 1024
PASSES = 2
BLOCKS_GROUP = 8
CAP = 64
SLOTS = 2048
ROWS = 32768
CENTROIDS = 32768
N_DP = 4
N_BLK = 8
DEVICES = 32


def steps_of(stream_key, dims, shards, least, high):
    loudness, own = 1.0, jax.random.fold_in(stream_key, 6)
    for axis_at, blocks in shards:
        heights = jnp.exp(jax.random.uniform(jax.random.fold_in(own, axis_at), (blocks,), jnp.float32, least / len(shards), high / len(shards)))
        loudness = loudness * jnp.repeat(heights, dims[axis_at] // blocks).reshape([-1 if axis == axis_at else 1 for axis in range(len(dims))])
    return loudness


def deal_out(stream_key, own, number, rows, number_of, top, bound, slope):
    sequence = jax.random.permutation(stream_key, number_of)
    heavy_load, ordinary = portions_of(number_of, rows * top, bound, slope, True), portions_of(number_of, rows * top, bound, slope, False)
    places = jnp.arange(number_of)

    def named(sizes, turn):
        used = int((sizes > 0).sum())
        fixed = max(1, used // 4)
        shifted = fixed + (places - fixed + turn * (used - fixed)) % max(1, number_of - fixed)
        return jnp.zeros((number_of,), jnp.int32).at[sequence[jnp.where(places < fixed, places, shifted)]].set(jnp.asarray(sizes, jnp.int32))

    sizes = jnp.where(number % 4 == 0, named(heavy_load, number // 4), named(ordinary, number - number // 4 - 1))
    mixed = jax.random.permutation(jax.random.fold_in(own, 3), number_of)
    source_of, receiver = mixed[0:number_of // 2 * 2:2], mixed[1:number_of // 2 * 2:2]
    margin = jnp.minimum(sizes[source_of] - 1, bound - sizes[receiver]) // 2
    margin = jnp.where((source_of == sequence[0]) | (receiver == sequence[0]) | (sizes[receiver] == 0), 0, jnp.maximum(margin, 0))
    shifted = jax.random.randint(jax.random.fold_in(own, 4), (number_of // 2,), 0, 1 << 20) % (margin + 1)
    sizes = sizes.at[source_of].add(-shifted).at[receiver].add(shifted)
    items = jnp.searchsorted(jnp.cumsum(sizes), jnp.arange(rows * top), side="right").astype(jnp.int32)
    listing = items.reshape(top, rows).T
    listing = listing[jax.random.permutation(jax.random.fold_in(own, 1), rows)]
    turn = jax.random.randint(jax.random.fold_in(own, 2), (rows, 1), 0, top)
    return jnp.take_along_axis(listing, (jnp.arange(top)[None, :] + turn) % top, axis=1)


def portions_of(amount, total, most, slope, full):
    loads = [(1 << 20) // math.isqrt(rank ** slope) + 1 for rank in range(1, amount + 1)]
    largest = most if full else min(most, max(-(-total // amount), total * loads[0] // sum(loads)))
    least = 1 if total - largest >= amount - 1 else 0
    given, rest = [largest] + [least] * (amount - 1), total - largest - least * (amount - 1)
    while rest > 0:
        candidates = [i for i in range(1, amount) if given[i] < largest] or [i for i in range(1, amount) if given[i] < most]
        mass, remaining = sum([loads[i] for i in candidates]), rest
        for i in candidates:
            addition = min(most - given[i], max(1, remaining * loads[i] // mass), rest)
            given[i] = given[i] + addition
            rest = rest - addition
    return np.array(given)


def centred(own_key, shape, width, most, shards=(), kind=jnp.bfloat16):
    entries = width * jax.random.normal(own_key, shape, jnp.float32)
    if shards:
        entries = entries * steps_of(own_key, shape, shards, -0.22, 0.18)
    return jnp.clip(entries, -most, most).astype(kind)


def setup_inputs(seed: int = 0) -> dict:
    key_of = jax.random.split(jax.random.key(seed), 5)
    rows = centred(key_of[0], (ROWS, D), 1.0, 6.0, ((0, 32),))
    block_ids_keys = jax.random.split(jax.random.fold_in(key_of[1], 1), ROWS // ROWS_DEV)
    block_ids_turns = jax.random.permutation(jax.random.fold_in(key_of[1], 3), ROWS // ROWS_DEV)
    block_ids = jax.vmap(lambda own, number: deal_out(jax.random.fold_in(key_of[1], 2), own, number, ROWS_DEV, DEVICES, 1, CAP, 1))(block_ids_keys, block_ids_turns).reshape((ROWS, 1))
    centroids = centred(key_of[2], (CENTROIDS, D), 1.0, 6.0, ((0, 32),), jnp.float32)
    pairing = jax.random.randint(key_of[3], (PASSES,), 1, N_BLK).astype(jnp.int32)
    return {"rows": rows, "block_ids": block_ids, "centroids": centroids, "pairing": pairing}


KAPPA = 64.0

def unit_vectors(values):
    wide = values.astype(jnp.float32)
    scale = lax.rsqrt(lax.optimization_barrier(jnp.mean(wide * wide, axis=-1, keepdims=True)) + 1e-06) * values.shape[-1] ** (-0.5)
    return (wide * scale).astype(jnp.bfloat16)

def reference(rows, block_ids, centroids, pairing):
    devices = N_DP * N_BLK
    owners = block_ids[:, 0].astype(jnp.int32)
    source = jnp.arange(ROWS, dtype=jnp.int32) // ROWS_DEV
    indicator = (owners[:, None] == jnp.arange(devices, dtype=jnp.int32)[None, :]).astype(jnp.int32)
    grouped = indicator.reshape(devices, ROWS_DEV, devices)
    earlier = (jnp.cumsum(grouped, axis=1, dtype=jnp.int32) - grouped).reshape(ROWS, devices)
    position = (source * CAP + lax.optimization_barrier(jnp.sum(earlier * indicator, axis=1, dtype=jnp.int32))).astype(jnp.int32)
    unit_rows = unit_vectors(rows)
    slot_rows = jnp.zeros((devices, SLOTS, D), jnp.bfloat16).at[owners, position].set(unit_rows)
    present = jnp.zeros((devices, SLOTS), jnp.float32).at[owners, position].set(1.0)
    blocks = jnp.arange(devices, dtype=jnp.int32)
    group_base = blocks // BLOCKS_GROUP * BLOCKS_GROUP
    inside = blocks % BLOCKS_GROUP
    tiles = centroids.reshape(devices, C_DEV, D).astype(jnp.float32)
    last_totals = jnp.zeros((devices, SLOTS), jnp.float32)
    for pass_index in range(PASSES):
        unit_tiles = unit_vectors(tiles)
        partner = (group_base + jnp.bitwise_xor(inside, pairing[pass_index])).astype(jnp.int32)

        def one_block(block):
            slot_block = slot_rows[block]
            marks = present[block]
            stacked = jnp.concatenate([unit_tiles[block], unit_tiles[partner[block]]], axis=0)
            affinity = jnp.exp(KAPPA * jnp.dot(slot_block, stacked.T, preferred_element_type=jnp.float32)) * marks[:, None]
            totals = lax.optimization_barrier(jnp.sum(affinity, axis=1))
            weights = (affinity / (totals + 1.0 - marks)[:, None]).astype(jnp.bfloat16)
            sums = jnp.dot(weights.T, slot_block, preferred_element_type=jnp.float32)
            column_sums = lax.optimization_barrier(jnp.sum(weights.astype(jnp.float32), axis=0))
            return (sums[:C_DEV], sums[C_DEV:].astype(jnp.bfloat16), column_sums[:C_DEV], column_sums[C_DEV:].astype(jnp.bfloat16), totals)
        own_sums, part_sums, own_counts, part_counts, totals = lax.map(one_block, blocks)
        part_sums = lax.optimization_barrier(part_sums)
        part_counts = lax.optimization_barrier(part_counts)
        numerator = own_sums + part_sums[partner].astype(jnp.float32)
        counts = own_counts + part_counts[partner].astype(jnp.float32)
        tiles = D ** 0.5 * (numerator + unit_tiles.astype(jnp.float32)) / (counts + 1.0)[:, :, None]
        last_totals = totals
    energy = jnp.log(last_totals[owners, position] / (2.0 * C_DEV))
    return (tiles.reshape(CENTROIDS, D), energy)
```

```python
import functools
import math

import jax
import jax.numpy as jnp
from jax import lax
from jax.experimental import pallas as pl
from jax.experimental.pallas import tpu as pltpu
from jax.sharding import PartitionSpec as P

PASSES = 2
PIECES = 2
KAPPA = 64.0
BLOCK = 256
VMEM_BYTES = 32 * 1024 * 1024


def unit_vectors(values):
    wide = values.astype(jnp.float32)
    scale = lax.rsqrt(jnp.mean(wide * wide, axis=-1, keepdims=True) + 1e-06) * values.shape[-1] ** (
        -0.5
    )
    return (wide * scale).astype(jnp.bfloat16)


def contract_rows(left, right):
    return lax.dot_general(
        left, right, (((1,), (1,)), ((), ())), preferred_element_type=jnp.float32
    )


def contract_slots(left, right):
    return lax.dot_general(
        left, right, (((0,), (0,)), ((), ())), preferred_element_type=jnp.float32
    )


def swapped(value, mask):
    return lax.ppermute(value, "blk", [(i, i ^ mask) for i in range(lax.axis_size("blk"))])


def pieces_of(tile_rows):
    piece = tile_rows // PIECES
    return [slice(at * piece, (at + 1) * piece) for at in range(PIECES)]


def exchange_all(value):
    return lax.all_to_all(value, ("dp", "blk"), split_axis=0, concat_axis=0, tiled=True)


def place_rows(rows, block_ids):
    devices = lax.axis_size("dp") * lax.axis_size("blk")
    rows_dev, width = rows.shape
    capacity = 2 * rows_dev // devices
    slot_count = devices * capacity
    owners = block_ids[:, 0]
    named = owners[:, None] == jnp.arange(devices, dtype=jnp.int32)[None, :]
    indicator = named.astype(jnp.bfloat16)
    order = jnp.arange(rows_dev, dtype=jnp.int32)
    before = (order[:, None] > order[None, :]).astype(jnp.bfloat16)
    earlier = jnp.dot(before, indicator, preferred_element_type=jnp.float32)
    rank = jnp.sum(jnp.where(named, earlier, 0.0), axis=1).astype(jnp.int32)
    position = owners * capacity + rank
    loads = jnp.sum(named.astype(jnp.float32), axis=0).astype(jnp.bfloat16)
    loads = exchange_all(jnp.broadcast_to(loads[:, None], (devices, 128)))
    chosen = jnp.arange(slot_count, dtype=jnp.int32)[:, None] == position[None, :]
    outgoing = jnp.dot(
        chosen.astype(jnp.bfloat16), unit_vectors(rows), preferred_element_type=jnp.float32
    ).astype(jnp.bfloat16)
    within = jnp.arange(capacity, dtype=jnp.int32)[None, :].astype(jnp.float32)
    present = (within < loads[:, :1].astype(jnp.float32)).astype(jnp.float32)
    return outgoing.reshape(devices, capacity, width), present.reshape(1, slot_count), position


def score_kernel(tiles_ref, rows_ref, marks_ref, affinity_ref, totals_ref):
    slots = rows_ref.shape[0]
    chunk = min(512, slots)

    @pl.when(pl.program_id(0) == 0)
    def _():
        totals_ref[...] = jnp.zeros_like(totals_ref)

    @pl.loop(0, slots // chunk)
    def _(at):
        span = pl.ds(pl.multiple_of(at * chunk, chunk), chunk)
        scores = contract_rows(tiles_ref[...], rows_ref[span, :])
        affinity = jnp.exp(KAPPA * scores) * marks_ref[:, span]
        affinity_ref[:, span] = affinity
        totals_ref[:, span] += jnp.sum(affinity, axis=0, keepdims=True)


def sums_kernel(affinity_ref, rows_ref, scale_ref, sums_ref, counts_ref, held):
    slots = rows_ref.shape[0]
    chunk = min(512, slots)
    held[...] = jnp.zeros_like(held)
    counts_ref[...] = jnp.zeros_like(counts_ref)

    @pl.loop(0, slots // chunk)
    def _(at):
        span = pl.ds(pl.multiple_of(at * chunk, chunk), chunk)
        weights = (affinity_ref[:, span] * scale_ref[:, span]).astype(jnp.bfloat16)
        held[...] += jnp.dot(weights, rows_ref[span, :], preferred_element_type=jnp.float32)
        counts_ref[...] += jnp.sum(weights.astype(jnp.float32), axis=1, keepdims=True)

    sums_ref[...] = held[...].astype(sums_ref.dtype)


def score(tiles, slot_block, marks):
    count, width = tiles.shape
    slots = slot_block.shape[0]
    block = min(BLOCK, count)
    return pl.pallas_call(
        score_kernel,
        grid=(count // block,),
        in_specs=[
            pl.BlockSpec((block, width), lambda i: (i, 0)),
            pl.BlockSpec((slots, width), lambda i: (0, 0)),
            pl.BlockSpec((1, slots), lambda i: (0, 0)),
        ],
        out_specs=[
            pl.BlockSpec((block, slots), lambda i: (i, 0)),
            pl.BlockSpec((1, slots), lambda i: (0, 0)),
        ],
        out_shape=[
            jax.ShapeDtypeStruct((count, slots), jnp.float32),
            jax.ShapeDtypeStruct((1, slots), jnp.float32),
        ],
        compiler_params=pltpu.CompilerParams(vmem_limit_bytes=VMEM_BYTES),
        cost_estimate=pl.CostEstimate(
            flops=2 * count * slots * width,
            bytes_accessed=2 * width * (slots + count) + 4 * count * slots,
            transcendentals=count * slots,
        ),
    )(tiles, slot_block, marks)


def weigh(affinity, slot_block, scale, kind):
    count, slots = affinity.shape
    width = slot_block.shape[1]
    block = min(BLOCK, count)
    return pl.pallas_call(
        sums_kernel,
        grid=(count // block,),
        in_specs=[
            pl.BlockSpec((block, slots), lambda i: (i, 0)),
            pl.BlockSpec((slots, width), lambda i: (0, 0)),
            pl.BlockSpec((1, slots), lambda i: (0, 0)),
        ],
        out_specs=[
            pl.BlockSpec((block, width), lambda i: (i, 0)),
            pl.BlockSpec((block, 1), lambda i: (i, 0)),
        ],
        out_shape=[
            jax.ShapeDtypeStruct((count, width), kind),
            jax.ShapeDtypeStruct((count, 1), jnp.float32),
        ],
        scratch_shapes=[pltpu.VMEM((block, width), jnp.float32)],
        compiler_params=pltpu.CompilerParams(vmem_limit_bytes=VMEM_BYTES),
        cost_estimate=pl.CostEstimate(
            flops=2 * count * slots * width,
            bytes_accessed=2 * width * (slots + 2 * count) + 4 * count * slots,
            transcendentals=0,
        ),
    )(affinity, slot_block, scale)


def one_pass(mask, unit_tiles, partner_pieces, slot_block, marks):
    own, totals = score(unit_tiles, slot_block, marks)
    partner = []
    for piece in partner_pieces:
        affinity, part = score(piece, slot_block, marks)
        partner.append(affinity)
        totals = totals + part
    divisor = totals + 1.0 - marks
    scale = 1.0 / divisor
    back_counts, back_sums = [], []
    for affinity in partner:
        sums, counts = weigh(affinity, slot_block, scale, jnp.bfloat16)
        back_sums.append(swapped(sums, mask))
        back_counts.append(swapped(counts[:, 0].astype(jnp.bfloat16), mask))
    own_sums, own_counts = weigh(own, slot_block, scale, jnp.float32)
    return (own_sums, own_counts, back_sums, back_counts), divisor


def new_centers(unit_tiles, parts):
    own_sums, own_counts, back_sums, back_counts = parts
    width = own_sums.shape[1]
    numerator = own_sums + jnp.concatenate(back_sums, axis=0).astype(jnp.float32)
    counts = own_counts[:, 0] + jnp.concatenate(back_counts, axis=0).astype(jnp.float32)
    return (
        math.sqrt(width)
        * (numerator + unit_tiles.astype(jnp.float32))
        / (counts + 1.0)[:, None]
    )


def partner_tiles(unit_tiles, mask):
    return [swapped(unit_tiles[span], mask) for span in pieces_of(unit_tiles.shape[0])]


def first_pass(mask, unit_tiles, outgoing, marks):
    partner_pieces = partner_tiles(unit_tiles, mask)
    slot_block = exchange_all(outgoing).reshape(-1, outgoing.shape[-1])
    parts, _ = one_pass(mask, unit_tiles, partner_pieces, slot_block, marks)
    return parts, slot_block


def last_pass(mask, unit_tiles, slot_block, marks):
    devices = lax.axis_size("dp") * lax.axis_size("blk")
    partner_pieces = partner_tiles(unit_tiles, mask)
    parts, divisor = one_pass(mask, unit_tiles, partner_pieces, slot_block, marks)
    slot_energy = jnp.log(divisor / (2.0 * unit_tiles.shape[0]))
    return parts, exchange_all(slot_energy.reshape(devices, -1)).reshape(-1)


def on_device(rows, block_ids, centroids, pairing):
    masks = range(1, lax.axis_size("blk"))
    unit_tiles = unit_vectors(centroids)
    outgoing, marks, position = place_rows(rows, block_ids)
    parts, slot_block = lax.switch(
        pairing[0] - 1,
        [functools.partial(first_pass, mask) for mask in masks],
        unit_tiles,
        outgoing,
        marks,
    )
    unit_tiles = unit_vectors(new_centers(unit_tiles, parts))
    parts, returned = lax.switch(
        pairing[1] - 1,
        [functools.partial(last_pass, mask) for mask in masks],
        unit_tiles,
        slot_block,
        marks,
    )
    chosen = jnp.arange(returned.shape[0], dtype=jnp.int32)[None, :] == position[:, None]
    energy = jnp.sum(jnp.where(chosen, returned[None, :], 0.0), axis=1)
    return new_centers(unit_tiles, parts), energy


def solution(mesh):
    in_specs = (P(("dp", "blk"), None), P(("dp", "blk"), None), P(("dp", "blk"), None), P())
    out_specs = (P(("dp", "blk"), None), P(("dp", "blk")))
    return jax.shard_map(
        on_device, mesh=mesh, in_specs=in_specs, out_specs=out_specs, check_vma=False
    )
```

```python
import functools
import math

import jax
import jax.numpy as jnp
from jax import lax
from jax.experimental import pallas as pl
from jax.experimental.pallas import tpu as pltpu
from jax.sharding import PartitionSpec as P

PASSES = 2
PIECES = 2
KAPPA = 64.0
BLOCK = 256
VMEM_BYTES = 32 * 1024 * 1024


def unit_vectors(values):
    wide = values.astype(jnp.float32)
    scale = lax.rsqrt(jnp.mean(wide * wide, axis=-1, keepdims=True) + 1e-06) * values.shape[-1] ** (
        -0.5
    )
    return (wide * scale).astype(jnp.bfloat16)


def contract_rows(left, right):
    return lax.dot_general(
        left, right, (((1,), (1,)), ((), ())), preferred_element_type=jnp.float32
    )


def contract_slots(left, right):
    return lax.dot_general(
        left, right, (((0,), (0,)), ((), ())), preferred_element_type=jnp.float32
    )


def swapped(value, mask):
    return lax.ppermute(value, "blk", [(i, i ^ mask) for i in range(lax.axis_size("blk"))])


def pieces_of(tile_rows):
    piece = tile_rows // PIECES
    return [slice(at * piece, (at + 1) * piece) for at in range(PIECES)]


def exchange_all(value):
    return lax.all_to_all(value, ("dp", "blk"), split_axis=0, concat_axis=0, tiled=True)


def place_rows(rows, block_ids):
    devices = lax.axis_size("dp") * lax.axis_size("blk")
    rows_dev, width = rows.shape
    capacity = 2 * rows_dev // devices
    slot_count = devices * capacity
    owners = block_ids[:, 0]
    named = owners[:, None] == jnp.arange(devices, dtype=jnp.int32)[None, :]
    indicator = named.astype(jnp.bfloat16)
    order = jnp.arange(rows_dev, dtype=jnp.int32)
    before = (order[:, None] > order[None, :]).astype(jnp.bfloat16)
    earlier = jnp.dot(before, indicator, preferred_element_type=jnp.float32)
    rank = jnp.sum(jnp.where(named, earlier, 0.0), axis=1).astype(jnp.int32)
    position = owners * capacity + rank
    loads = jnp.sum(named.astype(jnp.float32), axis=0).astype(jnp.bfloat16)
    loads = exchange_all(jnp.broadcast_to(loads[:, None], (devices, 128)))
    chosen = jnp.arange(slot_count, dtype=jnp.int32)[:, None] == position[None, :]
    outgoing = jnp.dot(
        chosen.astype(jnp.bfloat16), unit_vectors(rows), preferred_element_type=jnp.float32
    ).astype(jnp.bfloat16)
    within = jnp.arange(capacity, dtype=jnp.int32)[None, :].astype(jnp.float32)
    present = (within < loads[:, :1].astype(jnp.float32)).astype(jnp.float32)
    return outgoing.reshape(devices, capacity, width), present.reshape(1, slot_count), position


def score_kernel(tiles_ref, rows_ref, marks_ref, affinity_ref, totals_ref):
    slots = rows_ref.shape[0]
    chunk = min(512, slots)

    @pl.when(pl.program_id(0) == 0)
    def _():
        totals_ref[...] = jnp.zeros_like(totals_ref)

    @pl.loop(0, slots // chunk)
    def _(at):
        span = pl.ds(pl.multiple_of(at * chunk, chunk), chunk)
        scores = contract_rows(tiles_ref[...], rows_ref[span, :])
        affinity = jnp.exp(KAPPA * scores) * marks_ref[:, span]
        affinity_ref[:, span] = affinity
        totals_ref[:, span] += jnp.sum(affinity, axis=0, keepdims=True)


def sums_kernel(affinity_ref, rows_ref, scale_ref, sums_ref, counts_ref, held):
    slots = rows_ref.shape[0]
    chunk = min(512, slots)
    held[...] = jnp.zeros_like(held)
    counts_ref[...] = jnp.zeros_like(counts_ref)

    @pl.loop(0, slots // chunk)
    def _(at):
        span = pl.ds(pl.multiple_of(at * chunk, chunk), chunk)
        weights = (affinity_ref[:, span] * scale_ref[:, span]).astype(jnp.bfloat16)
        held[...] += jnp.dot(weights, rows_ref[span, :], preferred_element_type=jnp.float32)
        counts_ref[...] += jnp.sum(weights.astype(jnp.float32), axis=1, keepdims=True)

    sums_ref[...] = held[...].astype(sums_ref.dtype)


def score(tiles, slot_block, marks):
    count, width = tiles.shape
    slots = slot_block.shape[0]
    block = min(BLOCK, count)
    return pl.pallas_call(
        score_kernel,
        grid=(count // block,),
        in_specs=[
            pl.BlockSpec((block, width), lambda i: (i, 0)),
            pl.BlockSpec((slots, width), lambda i: (0, 0)),
            pl.BlockSpec((1, slots), lambda i: (0, 0)),
        ],
        out_specs=[
            pl.BlockSpec((block, slots), lambda i: (i, 0)),
            pl.BlockSpec((1, slots), lambda i: (0, 0)),
        ],
        out_shape=[
            jax.ShapeDtypeStruct((count, slots), jnp.float32),
            jax.ShapeDtypeStruct((1, slots), jnp.float32),
        ],
        compiler_params=pltpu.CompilerParams(vmem_limit_bytes=VMEM_BYTES),
        cost_estimate=pl.CostEstimate(
            flops=2 * count * slots * width,
            bytes_accessed=2 * width * (slots + count) + 4 * count * slots,
            transcendentals=count * slots,
        ),
    )(tiles, slot_block, marks)


def weigh(affinity, slot_block, scale, kind):
    count, slots = affinity.shape
    width = slot_block.shape[1]
    block = min(BLOCK, count)
    return pl.pallas_call(
        sums_kernel,
        grid=(count // block,),
        in_specs=[
            pl.BlockSpec((block, slots), lambda i: (i, 0)),
            pl.BlockSpec((slots, width), lambda i: (0, 0)),
            pl.BlockSpec((1, slots), lambda i: (0, 0)),
        ],
        out_specs=[
            pl.BlockSpec((block, width), lambda i: (i, 0)),
            pl.BlockSpec((block, 1), lambda i: (i, 0)),
        ],
        out_shape=[
            jax.ShapeDtypeStruct((count, width), kind),
            jax.ShapeDtypeStruct((count, 1), jnp.float32),
        ],
        scratch_shapes=[pltpu.VMEM((block, width), jnp.float32)],
        compiler_params=pltpu.CompilerParams(vmem_limit_bytes=VMEM_BYTES),
        cost_estimate=pl.CostEstimate(
            flops=2 * count * slots * width,
            bytes_accessed=2 * width * (slots + 2 * count) + 4 * count * slots,
            transcendentals=0,
        ),
    )(affinity, slot_block, scale)


def one_pass(mask, unit_tiles, partner_pieces, slot_block, marks):
    own, totals = score(unit_tiles, slot_block, marks)
    partner = []
    for piece in partner_pieces:
        affinity, part = score(piece, slot_block, marks)
        partner.append(affinity)
        totals = totals + part
    divisor = totals + 1.0 - marks
    scale = 1.0 / divisor
    back_counts, back_sums = [], []
    for affinity in partner:
        sums, counts = weigh(affinity, slot_block, scale, jnp.bfloat16)
        back_sums.append(swapped(sums, mask))
        back_counts.append(swapped(counts[:, 0].astype(jnp.bfloat16), mask))
    own_sums, own_counts = weigh(own, slot_block, scale, jnp.float32)
    return (own_sums, own_counts, back_sums, back_counts), divisor


def new_centers(unit_tiles, parts):
    own_sums, own_counts, back_sums, back_counts = parts
    width = own_sums.shape[1]
    numerator = own_sums + jnp.concatenate(back_sums, axis=0).astype(jnp.float32)
    counts = own_counts[:, 0] + jnp.concatenate(back_counts, axis=0).astype(jnp.float32)
    return (
        math.sqrt(width)
        * (numerator + unit_tiles.astype(jnp.float32))
        / (counts + 1.0)[:, None]
    )


def partner_tiles(unit_tiles, mask):
    return [swapped(unit_tiles[span], mask) for span in pieces_of(unit_tiles.shape[0])]


def first_pass(mask, unit_tiles, outgoing, marks):
    partner_pieces = partner_tiles(unit_tiles, mask)
    slot_block = exchange_all(outgoing).reshape(-1, outgoing.shape[-1])
    parts, _ = one_pass(mask, unit_tiles, partner_pieces, slot_block, marks)
    return parts, slot_block


def last_pass(mask, unit_tiles, slot_block, marks):
    partner_pieces = partner_tiles(unit_tiles, mask)
    return one_pass(mask, unit_tiles, partner_pieces, slot_block, marks)


def on_device(rows, block_ids, centroids, pairing):
    masks = range(1, lax.axis_size("blk"))
    unit_tiles = unit_vectors(centroids)
    outgoing, marks, position = place_rows(rows, block_ids)
    parts, slot_block = lax.switch(
        pairing[0] - 1,
        [functools.partial(first_pass, mask) for mask in masks],
        unit_tiles,
        outgoing,
        marks,
    )
    unit_tiles = unit_vectors(new_centers(unit_tiles, parts))
    parts, divisor = lax.switch(
        pairing[1] - 1,
        [functools.partial(last_pass, mask) for mask in masks],
        unit_tiles,
        slot_block,
        marks,
    )
    devices = lax.axis_size("dp") * lax.axis_size("blk")
    slot_energy = jnp.log(divisor / (2.0 * unit_tiles.shape[0]))
    returned = exchange_all(slot_energy.reshape(devices, -1)).reshape(-1)
    chosen = jnp.arange(returned.shape[0], dtype=jnp.int32)[None, :] == position[:, None]
    energy = jnp.sum(jnp.where(chosen, returned[None, :], 0.0), axis=1)
    return new_centers(unit_tiles, parts), energy


def solution(mesh):
    in_specs = (P(("dp", "blk"), None), P(("dp", "blk"), None), P(("dp", "blk"), None), P())
    out_specs = (P(("dp", "blk"), None), P(("dp", "blk")))
    return jax.shard_map(
        on_device, mesh=mesh, in_specs=in_specs, out_specs=out_specs, check_vma=False
    )
```
